32 devices in a mesh: groups: 2 (over y), tensor: 4 (over z), dp: 2 (over x), pipe: 2 (over core).
Axes of the slice: x: 2, y: 2, z: 4, core: 2. Of those that a mesh axis runs over, the one named last changes fastest.
Arguments:
- tokens: bfloat16 [512, 16384], P(('groups', 'dp', 'pipe'), 'tensor'), parts along dimension 0, may hold values from -6 to 6
- signs: int32 [16384], P('tensor'), may hold values from -1 to 1, as said below
- exponents: int32 [512], P(('groups', 'dp', 'pipe')), parts along dimension 0, may hold values from -12 to 0
- weights: bfloat16 [16384, 18432], P('tensor', ('dp', 'pipe')), may hold values from -0.046875 to 0.046875
Outputs:
- projected: bfloat16 [512, 18432], P(('groups', 'tensor'), ('dp', 'pipe')), parts along dimension 0
The draws below stay inside these ranges and needn't reach their ends.
There are 2 independent parts, one for each index of `groups`. The reference program is written for one: setup_inputs(seed, part) draws one part's arguments, and reference() takes and returns one part's arrays. A program takes and returns all parts, laid end to end along the dimension named above; an argument that names none is the same for every part. Nothing has to cross between parts.
Inputs may be any that keep to these rules, and one draw needn't show every extreme that they name: `signs`: each entry is -1 or 1.
All inputs are finite; a program needn't handle non-finite values.
Results may differ from the reference program's by a relative error of at most 0.015.
Values may be sent and summed in bfloat16 or wider, within the bound.
A program may use at most 128 MiB of HBM per device.

```python
import math
import jax
import jax.numpy as jnp
from jax import lax

D = 16384
QKV = 18432
TOKENS = 256
N_TENSOR = 4


def draw_signs(key, part):
    key = jax.random.fold_in(key, 11)
    return (2 * jax.random.randint(key, (D,), 0, 2) - 1).astype(jnp.int32)


def plant(values, key, low, high):
    spot = [jax.random.randint(jax.random.fold_in(key, axis), (), 0, length) for axis, length in enumerate(values.shape)]
    widest = values.shape.index(max(values.shape))
    neighbour = spot[:widest] + [(spot[widest] + 1) % values.shape[widest]] + spot[widest + 1:]
    return values.at[tuple(spot)].set(low).at[tuple(neighbour)].set(high)


def block_scale(own_key, shape, split, low, largest):
    gain = 1.0
    for position, shards_of in split:
        heights = jax.random.uniform(jax.random.fold_in(jax.random.fold_in(own_key, 6), position), (shards_of,), jnp.float32, low / len(split), largest / len(split))
        gain = gain * jnp.repeat(jnp.exp(heights), shape[position] // shards_of).reshape((-1,) + (1,) * (len(shape) - 1 - position))
    return gain


def scatter_about(rng, shape, spread, most, shards=(), kind=jnp.bfloat16):
    entries = jax.random.normal(rng, shape, jnp.float32) * spread
    if len(shards) > 0:
        entries = block_scale(rng, shape, shards, -0.22, 0.18) * entries
    return jnp.clip(entries, min=-most, max=most).astype(kind)


def setup_inputs(seed: int = 0, part: int = 0) -> dict:
    key_of = jax.random.split(jax.random.key(seed), 5)
    part_keys = jax.random.split(jax.random.fold_in(key_of[4], part), 5)
    return {
        "tokens": scatter_about(part_keys[0], (TOKENS, D), 1.0, 6.0, ((0, 4), (1, 4))),
        "signs": draw_signs(jax.random.fold_in(key_of[4], 71), part),
        "exponents": plant(jax.random.randint(part_keys[2], (TOKENS,), -12, 1), jax.random.fold_in(part_keys[2], 1), -12, 0).astype(jnp.int32),
        "weights": scatter_about(key_of[3], (D, QKV), D ** -0.5, 0.046875, ((0, 4), (1, 4))),
    }


def sylvester(order):
    rows = jnp.arange(order, dtype=jnp.int32)[:, None]
    cols = jnp.arange(order, dtype=jnp.int32)[None, :]
    parity = jnp.zeros((order, order), jnp.int32)
    for level in range(order.bit_length() - 1):
        parity = parity + rows // 2 ** level % 2 * (cols // 2 ** level % 2)
    return (1 - 2 * (parity % 2)).astype(jnp.float32)

def reference(tokens, signs, exponents, weights):
    count = tokens.shape[0]
    levels = D.bit_length() - 1
    high = 2 ** (levels // 2)
    low = D // high
    signed = tokens.astype(jnp.float32) * signs.astype(jnp.float32)[None, :]
    folded = signed.reshape(count, high, low)
    folded = jnp.einsum('tab,bj->taj', folded, sylvester(low), precision=lax.Precision.HIGHEST)
    folded = jnp.einsum('taj,ai->tij', folded, sylvester(high), precision=lax.Precision.HIGHEST)
    rotated = folded.reshape(count, D) * jnp.float32(1.0 / math.sqrt(D))
    scale = jnp.exp2(jnp.float32(0.25) * exponents.astype(jnp.float32))[:, None]
    level = rotated / scale
    soft = jnp.clip(level - jnp.sin(2.0 * math.pi * level) / (2.0 * math.pi), -8.0, 7.0)
    quantized = (soft * scale).astype(jnp.bfloat16)
    width = D // N_TENSOR
    blocks = quantized.reshape(count, N_TENSOR, width).transpose(1, 0, 2)
    weight_blocks = weights.reshape(N_TENSOR, width, QKV)

    def accumulate(total, pair):
        part = jnp.dot(pair[0], pair[1], preferred_element_type=jnp.float32)
        part = lax.optimization_barrier(part.astype(jnp.bfloat16)).astype(jnp.float32)
        return (total + part, None)
    total, unused = lax.scan(accumulate, jnp.zeros((count, QKV), jnp.float32), (blocks, weight_blocks))
    return total.astype(jnp.bfloat16)
```

```python
import functools
import math

import jax
import jax.numpy as jnp
from jax import lax
from jax.experimental import pallas as pl
from jax.experimental.pallas import tpu as pltpu
from jax.sharding import PartitionSpec as P

D = 16384
MESH = pl.DeviceIdType.MESH
BASE = 256
PARTS = 2


def partner_2(value, axis, bit):
    mask = 2**bit
    pairs = [(source, source ^ mask) for source in range(lax.axis_size(axis))]
    return lax.ppermute(value, axis, pairs)


def sylvester(order):
    rows = lax.broadcasted_iota(jnp.int32, (order, order), 0)
    cols = lax.broadcasted_iota(jnp.int32, (order, order), 1)
    both = rows & cols
    shift = 1
    while shift < order.bit_length():
        both = both ^ (both >> shift)
        shift *= 2
    return (1 - 2 * (both & 1)).astype(jnp.float32)


def butterfly(values):
    values = list(values)
    step = 1
    while step < len(values):
        for low in range(len(values)):
            if low & step == 0:
                a, b = values[low], values[low + step]
                values[low], values[low + step] = a + b, a - b
        step *= 2
    return values


def sin_turns(turns):
    part = turns - jnp.round(turns)
    part = jnp.where(part > 0.25, 0.5 - part, jnp.where(part < -0.25, -0.5 - part, part))
    angle = part * jnp.float32(2.0 * math.pi)
    square = angle * angle
    total = jnp.float32(-1.0 / math.factorial(11))
    for order, sign in ((9, 1.0), (7, -1.0), (5, 1.0), (3, -1.0)):
        total = total * square + jnp.float32(sign / math.factorial(order))
    return angle + angle * square * total


def fake_quantize(rotated, scale, inverse):
    level = rotated * inverse
    soft = jnp.clip(level - sin_turns(level) * jnp.float32(1.0 / (2.0 * math.pi)), -8.0, 7.0)
    return (soft * scale).astype(jnp.bfloat16)


def kernel(
    nz, strip, tokens, signs, exponents, weights, out,
    held, mixed, taken, levels, acts, terms, from_left, from_right,
    weight_sem, mix_send, mix_recv, lev_send, lev_recv, x_send, x_recv,
    core_send, core_recv, pass_send, pass_recv, right_send, right_recv, left_send, left_recv,
):
    rows, width = tokens.shape
    quarter = width // nz
    part_rows = rows // PARTS
    strips = weights.shape[1] // strip
    chunk = out.shape[0]
    z = lax.axis_index("tensor")
    x = lax.axis_index("dp")
    core = lax.axis_index("pipe")
    across = {"dp": 1 - x}
    beside = {"pipe": 1 - core}

    def weight_copy(s):
        return pltpu.make_async_copy(
            weights.at[:, pl.ds(pl.multiple_of(s * strip, strip), strip)], held.at[s], weight_sem.at[s]
        )

    barrier = pltpu.get_barrier_semaphore()
    for k in range(1, nz):
        pl.semaphore_signal(barrier, inc=1, device_id={"tensor": z ^ k}, device_id_type=MESH)
    pl.semaphore_signal(barrier, inc=1, device_id=across, device_id_type=MESH)
    pl.semaphore_signal(barrier, inc=1, device_id=beside, device_id_type=MESH)

    small = sylvester(BASE).astype(jnp.bfloat16)
    signed = signs[...].astype(jnp.bfloat16)

    def mix_copy(h, k):
        span = pl.ds(h * part_rows, part_rows)
        return pltpu.make_async_remote_copy(
            src_ref=mixed.at[z ^ k, span], dst_ref=taken.at[z, span],
            send_sem=mix_send.at[h, k], recv_sem=mix_recv.at[h, k],
            device_id={"tensor": z ^ k}, device_id_type=MESH,
        )

    for h in range(PARTS):
        span = slice(h * part_rows, (h + 1) * part_rows)
        blocks = []
        for a in range(width // BASE):
            cols = slice(a * BASE, (a + 1) * BASE)
            blocks.append(jnp.dot(tokens[span, cols] * signed[:, cols], small, preferred_element_type=jnp.float32))
        for a, block in enumerate(butterfly(blocks)):
            q, at = divmod(a * BASE, quarter)
            mixed[q, span, at:at + BASE] = (block * jnp.float32(1.0 / math.sqrt(D))).astype(jnp.bfloat16)
        if h == 0:
            pl.semaphore_wait(barrier, nz + 1)
        for k in range(nz - 1, 0, -1):
            mix_copy(h, k).start()
        taken[z, span] = mixed[z, span]

    pl.loop(0, strips)(lambda s: weight_copy(s).start())

    at_row = lax.broadcasted_iota(jnp.int32, (rows, rows), 0)
    at_col = lax.broadcasted_iota(jnp.int32, (rows, rows), 1)
    power = jnp.sum(
        jnp.where(at_row == at_col, 0.25 * exponents[...].astype(jnp.float32), 0.0), axis=1, keepdims=True
    )
    scale = jnp.exp2(power)
    inverse = jnp.exp2(-power)

    mine = (x * 2 + core) * rows

    def lev_copy(h, k):
        return pltpu.make_async_remote_copy(
            src_ref=levels.at[z ^ k, pl.ds(h * part_rows, part_rows)],
            dst_ref=acts.at[z, pl.ds(pl.multiple_of(mine + h * part_rows, part_rows), part_rows)],
            send_sem=lev_send.at[h, k], recv_sem=lev_recv.at[h, k],
            device_id={"tensor": z ^ k}, device_id_type=MESH,
        )

    def side_copy(h, k, owner_x, target, send, recv):
        at = (owner_x * 2 + core) * rows + h * part_rows
        ref = acts.at[z ^ k, pl.ds(pl.multiple_of(at, part_rows), part_rows)]
        return pltpu.make_async_remote_copy(
            src_ref=ref, dst_ref=ref, send_sem=send.at[h, k], recv_sem=recv.at[h, k],
            device_id=target, device_id_type=MESH,
        )

    def x_copy(h, k):
        return side_copy(h, k, x, across, x_send, x_recv)

    def core_copy(h, k):
        return side_copy(h, k, x, beside, core_send, core_recv)

    def pass_copy(h, k):
        return side_copy(h, k, 1 - x, beside, pass_send, pass_recv)

    for h in range(PARTS):
        span = slice(h * part_rows, (h + 1) * part_rows)
        for k in range(1, nz):
            mix_copy(h, k).wait_recv()
        for lane in range(0, quarter, BASE):
            lanes = slice(lane, lane + BASE)
            whole = butterfly([taken[q, span, lanes].astype(jnp.float32) for q in range(nz)])
            for q in range(nz):
                levels[q, span, lanes] = fake_quantize(whole[q], scale[span], inverse[span])
        for k in range(nz - 1, 0, -1):
            lev_copy(h, k).start()
        acts[z, pl.ds(pl.multiple_of(mine + h * part_rows, part_rows), part_rows)] = levels[z, span]
        x_copy(h, 0).start()
        core_copy(h, 0).start()

    steps = [(h, 0) for h in range(PARTS)] + [(h, k) for h in range(PARTS) for k in range(1, nz)]
    for i in range(len(steps) + 1):
        if PARTS <= i < len(steps):
            lev_copy(*steps[i]).wait_recv()
            x_copy(*steps[i]).start()
            core_copy(*steps[i]).start()
        if i > 0:
            x_copy(*steps[i - 1]).wait_recv()
            pass_copy(*steps[i - 1]).start()
    for step in steps:
        core_copy(*step).wait_recv()
        pass_copy(*step).wait_recv()

    def right_copy(s, d):
        return pltpu.make_async_remote_copy(
            src_ref=terms.at[s, d], dst_ref=from_left.at[s, d],
            send_sem=right_send.at[s, d], recv_sem=right_recv.at[s, d],
            device_id={"tensor": lax.rem(z + 1, nz)}, device_id_type=MESH,
        )

    def left_copy(s, d):
        return pltpu.make_async_remote_copy(
            src_ref=terms.at[s, d], dst_ref=from_right.at[s, d],
            send_sem=left_send.at[s, d], recv_sem=left_recv.at[s, d],
            device_id={"tensor": lax.rem(z + nz - 1, nz)}, device_id_type=MESH,
        )

    def add_in(s, d, arrived):
        terms[s, d] = (terms[s, d].astype(jnp.float32) + arrived[s, d].astype(jnp.float32)).astype(jnp.bfloat16)

    def when_strip(s, body):
        pl.when(jnp.logical_and(s >= 0, s < strips))(functools.partial(body, s))

    def multiply(s):
        weight_copy(s).wait()
        total = jnp.dot(acts[0], held[s, :quarter], preferred_element_type=jnp.float32)
        for q in range(1, nz):
            total += jnp.dot(
                acts[q], held[s, q * quarter:(q + 1) * quarter], preferred_element_type=jnp.float32
            )
        for d in range(nz):
            terms[s, d] = total[d * chunk:(d + 1) * chunk].astype(jnp.bfloat16)

    def hop(at, s):
        @pl.when(z == at)
        def _():
            for d in range(nz - 1, at, -1):
                if at > 0:
                    right_copy(s, d).wait_recv()
                    add_in(s, d, from_left)
                right_copy(s, d).start()

        @pl.when(z == nz - 1 - at)
        def _():
            for d in range(nz - 1 - at):
                if at > 0:
                    left_copy(s, d).wait_recv()
                    add_in(s, d, from_right)
                left_copy(s, d).start()

    def finish(s):
        cols = pl.ds(pl.multiple_of(s * strip, strip), strip)
        own = terms[s, z].astype(jnp.float32)

        @pl.when(z == 0)
        def _():
            left_copy(s, z).wait_recv()
            out[:, cols] = (own + from_right[s, z].astype(jnp.float32)).astype(out.dtype)

        @pl.when(z == nz - 1)
        def _():
            right_copy(s, z).wait_recv()
            out[:, cols] = (own + from_left[s, z].astype(jnp.float32)).astype(out.dtype)

        @pl.when(jnp.logical_and(z > 0, z < nz - 1))
        def _():
            right_copy(s, z).wait_recv()
            left_copy(s, z).wait_recv()
            out[:, cols] = (
                own + from_left[s, z].astype(jnp.float32) + from_right[s, z].astype(jnp.float32)
            ).astype(out.dtype)

    @pl.loop(0, strips + nz - 1)
    def _(t):
        when_strip(t, multiply)
        for at in range(nz - 1):
            when_strip(t - at, functools.partial(hop, at))
        when_strip(t - (nz - 1), finish)

    for h in range(PARTS):
        for k in range(nz):
            if k > 0:
                mix_copy(h, k).wait_send()
                lev_copy(h, k).wait_send()
            x_copy(h, k).wait_send()
            core_copy(h, k).wait_send()
            pass_copy(h, k).wait_send()

    @pl.loop(0, strips)
    def _(s):
        for d in range(nz):
            pl.when(z < d)(lambda d=d: right_copy(s, d).wait_send())
            pl.when(z > d)(lambda d=d: left_copy(s, d).wait_send())


def fused(nz, gathered, tokens, signs, exponents, weights):
    rows, width = tokens.shape
    depth, columns = weights.shape
    quarter = width // nz
    total = rows * gathered
    chunk = total // nz
    strip = next(s for s in (512, 256, 128) if columns % s == 0)
    strips = columns // strip
    vmem = pl.BlockSpec(memory_space=pltpu.VMEM)
    return pl.pallas_call(
        functools.partial(kernel, nz, strip),
        out_shape=jax.ShapeDtypeStruct((chunk, columns), jnp.bfloat16),
        in_specs=[vmem, vmem, vmem, pl.BlockSpec(memory_space=pl.ANY)],
        out_specs=vmem,
        scratch_shapes=[
            pltpu.VMEM((strips, depth, strip), jnp.bfloat16),
            pltpu.VMEM((nz, rows, quarter), jnp.bfloat16),
            pltpu.VMEM((nz, rows, quarter), jnp.bfloat16),
            pltpu.VMEM((nz, rows, quarter), jnp.bfloat16),
            pltpu.VMEM((nz, total, quarter), jnp.bfloat16),
            pltpu.VMEM((strips, nz, chunk, strip), jnp.bfloat16),
            pltpu.VMEM((strips, nz, chunk, strip), jnp.bfloat16),
            pltpu.VMEM((strips, nz, chunk, strip), jnp.bfloat16),
            pltpu.SemaphoreType.DMA((strips,)),
        ]
        + [pltpu.SemaphoreType.DMA((PARTS, nz))] * 10
        + [pltpu.SemaphoreType.DMA((strips, nz))] * 4,
        compiler_params=pltpu.CompilerParams(
            collective_id=0, has_side_effects=True, vmem_limit_bytes=60 * 2**20
        ),
        cost_estimate=pl.CostEstimate(
            flops=2 * total * depth * columns, bytes_accessed=2 * depth * columns, transcendentals=0
        ),
    )(tokens, signs[None, :], exponents[None, :], weights)


def shards(tokens, signs, exponents, weights):
    rows, width = tokens.shape
    members = lax.axis_size("tensor")
    gathered = lax.axis_size("dp") * lax.axis_size("pipe")
    if (
        lax.axis_size("dp") == 2 and lax.axis_size("pipe") == 2 and members > 1
        and width % (BASE * members) == 0 and rows % (16 * PARTS) == 0
        and rows * gathered % (16 * members) == 0 and weights.shape[1] % 128 == 0
        and 2 * width * weights.shape[1] <= 40 * 2**20
    ):
        return fused(members, gathered, tokens, signs, exponents, weights)
    signed = tokens * signs.astype(jnp.bfloat16)[None, :]
    mixed = jnp.dot(
        signed, sylvester(width).astype(jnp.bfloat16), preferred_element_type=jnp.float32
    )
    position = lax.axis_index("tensor")
    for level in range(members.bit_length() - 1):
        partner = partner_2(mixed.astype(jnp.bfloat16), "tensor", level).astype(mixed.dtype)
        upper = position // 2**level % 2
        mixed = jnp.where(upper == 0, mixed + partner, partner - mixed)
    rotated = mixed * jnp.float32(1.0 / math.sqrt(D))
    scale = jnp.exp2(jnp.float32(0.25) * exponents.astype(jnp.float32))[:, None]
    level_value = rotated / scale
    soft = jnp.clip(level_value - jnp.sin(2.0 * math.pi * level_value) / (2.0 * math.pi), -8.0, 7.0)
    quantized = (soft * scale).astype(jnp.bfloat16)
    terms = jnp.dot(
        lax.all_gather(quantized, ("dp", "pipe"), axis=0, tiled=True),
        weights,
        preferred_element_type=jnp.float32,
    )
    summed = lax.psum_scatter(terms.astype(jnp.bfloat16), "tensor", scatter_dimension=0, tiled=True)
    return summed


def solution(mesh):
    placed = (
        P(("groups", "dp", "pipe"), "tensor"),
        P("tensor"),
        P(("groups", "dp", "pipe")),
        P("tensor", ("dp", "pipe")),
    )
    return jax.shard_map(
        shards,
        mesh=mesh,
        in_specs=placed,
        out_specs=P(("groups", "tensor"), ("dp", "pipe")),
        check_vma=False,
    )
```

```python
import functools
import math

import jax
import jax.numpy as jnp
from jax import lax
from jax.experimental import pallas as pl
from jax.experimental.pallas import tpu as pltpu
from jax.sharding import PartitionSpec as P

D = 16384
MESH = pl.DeviceIdType.MESH
BASE = 256
PARTS = 2
CROSS_STEP = 0


def partner_2(value, axis, bit):
    mask = 2**bit
    pairs = [(source, source ^ mask) for source in range(lax.axis_size(axis))]
    return lax.ppermute(value, axis, pairs)


def sylvester(order):
    rows = lax.broadcasted_iota(jnp.int32, (order, order), 0)
    cols = lax.broadcasted_iota(jnp.int32, (order, order), 1)
    both = rows & cols
    shift = 1
    while shift < order.bit_length():
        both = both ^ (both >> shift)
        shift *= 2
    return (1 - 2 * (both & 1)).astype(jnp.float32)


def butterfly(values):
    values = list(values)
    step = 1
    while step < len(values):
        for low in range(len(values)):
            if low & step == 0:
                a, b = values[low], values[low + step]
                values[low], values[low + step] = a + b, a - b
        step *= 2
    return values


def sin_turns(turns):
    part = turns - jnp.round(turns)
    part = jnp.where(part > 0.25, 0.5 - part, jnp.where(part < -0.25, -0.5 - part, part))
    angle = part * jnp.float32(2.0 * math.pi)
    square = angle * angle
    total = jnp.float32(-1.0 / math.factorial(11))
    for order, sign in ((9, 1.0), (7, -1.0), (5, 1.0), (3, -1.0)):
        total = total * square + jnp.float32(sign / math.factorial(order))
    return angle + angle * square * total


def fake_quantize(rotated, scale, inverse):
    level = rotated * inverse
    soft = jnp.clip(level - sin_turns(level) * jnp.float32(1.0 / (2.0 * math.pi)), -8.0, 7.0)
    return (soft * scale).astype(jnp.bfloat16)


def kernel(
    nz, strip, tokens, signs, exponents, weights, out,
    held, mixed, taken, levels, acts, terms, from_left, from_right,
    weight_sem, mix_send, mix_recv, lev_send, lev_recv, x_send, x_recv,
    core_send, core_recv, pass_send, pass_recv, right_send, right_recv, left_send, left_recv,
):
    rows, width = tokens.shape
    quarter = width // nz
    part_rows = rows // PARTS
    strips = weights.shape[1] // strip
    z = lax.axis_index("tensor")
    x = lax.axis_index("dp")
    core = lax.axis_index("pipe")
    across = {"dp": 1 - x}
    beside = {"pipe": 1 - core}

    def weight_copy(s):
        return pltpu.make_async_copy(
            weights.at[:, pl.ds(pl.multiple_of(s * strip, strip), strip)], held.at[s], weight_sem.at[s]
        )

    barrier = pltpu.get_barrier_semaphore()
    for k in range(1, nz):
        pl.semaphore_signal(barrier, inc=1, device_id={"tensor": z ^ k}, device_id_type=MESH)
    pl.semaphore_signal(barrier, inc=1, device_id=across, device_id_type=MESH)
    pl.semaphore_signal(barrier, inc=1, device_id=beside, device_id_type=MESH)

    small = sylvester(BASE).astype(jnp.bfloat16)
    signed = signs[...].astype(jnp.bfloat16)

    def mix_copy(h, k):
        span = pl.ds(h * part_rows, part_rows)
        return pltpu.make_async_remote_copy(
            src_ref=mixed.at[z ^ k, span], dst_ref=taken.at[z, span],
            send_sem=mix_send.at[h, k], recv_sem=mix_recv.at[h, k],
            device_id={"tensor": z ^ k}, device_id_type=MESH,
        )

    def start_mix(h):
        for k in range(nz - 1, 0, -1):
            mix_copy(h, k).start()

    def mix(h):
        span = slice(h * part_rows, (h + 1) * part_rows)
        blocks = []
        for a in range(width // BASE):
            cols = slice(a * BASE, (a + 1) * BASE)
            blocks.append(jnp.dot(tokens[span, cols] * signed[:, cols], small, preferred_element_type=jnp.float32))
        for a, block in enumerate(butterfly(blocks)):
            q, at = divmod(a * BASE, quarter)
            mixed[q, span, at:at + BASE] = (block * jnp.float32(1.0 / math.sqrt(D))).astype(jnp.bfloat16)
        taken[z, span] = mixed[z, span]

    mix(0)
    pl.semaphore_wait(barrier, nz + 1)
    start_mix(0)
    pl.loop(0, strips)(lambda s: weight_copy(s).start())
    for h in range(1, PARTS):
        mix(h)

    at_row = lax.broadcasted_iota(jnp.int32, (rows, rows), 0)
    at_col = lax.broadcasted_iota(jnp.int32, (rows, rows), 1)
    power = jnp.sum(
        jnp.where(at_row == at_col, 0.25 * exponents[...].astype(jnp.float32), 0.0), axis=1, keepdims=True
    )
    scale = jnp.exp2(power)
    inverse = jnp.exp2(-power)

    def rows_of(owner_x):
        return pl.ds(pl.multiple_of((owner_x * 2 + core) * part_rows, part_rows), part_rows)

    def lev_copy(h, k):
        return pltpu.make_async_remote_copy(
            src_ref=levels.at[z ^ k, pl.ds(h * part_rows, part_rows)], dst_ref=acts.at[h, z, rows_of(x)],
            send_sem=lev_send.at[h, k], recv_sem=lev_recv.at[h, k],
            device_id={"tensor": z ^ k}, device_id_type=MESH,
        )

    def side_copy(h, k, owner_x, target, send, recv):
        ref = acts.at[h, z ^ k, rows_of(owner_x)]
        return pltpu.make_async_remote_copy(
            src_ref=ref, dst_ref=ref, send_sem=send.at[h, k], recv_sem=recv.at[h, k],
            device_id=target, device_id_type=MESH,
        )

    def x_copy(h, k):
        return side_copy(h, k, x, across, x_send, x_recv)

    def core_copy(h, k):
        return side_copy(h, k, x, beside, core_send, core_recv)

    def pass_copy(h, k):
        return side_copy(h, k, 1 - x, beside, pass_send, pass_recv)

    def cross(h):
        span = slice(h * part_rows, (h + 1) * part_rows)
        for k in range(1, nz):
            mix_copy(h, k).wait_recv()
        for lane in range(0, quarter, BASE):
            lanes = slice(lane, lane + BASE)
            whole = butterfly([taken[q, span, lanes].astype(jnp.float32) for q in range(nz)])
            for q in range(nz):
                levels[q, span, lanes] = fake_quantize(whole[q], scale[span], inverse[span])
        for k in range(nz - 1, 0, -1):
            lev_copy(h, k).start()
        acts[h, z, rows_of(x)] = levels[z, span]
        x_copy(h, 0).start()
        core_copy(h, 0).start()
        if h + 1 < PARTS:
            start_mix(h + 1)

    def gather(h, k):
        if k < nz:
            lev_copy(h, k).wait_recv()
            x_copy(h, k).start()
            core_copy(h, k).start()
        x_copy(h, k - 1).wait_recv()
        pass_copy(h, k - 1).start()
        if k == nz:
            for i in range(nz):
                core_copy(h, i).wait_recv()
                pass_copy(h, i).wait_recv()

    cross(0)
    for k in range(1, nz + 1):
        gather(0, k)

    def right_copy(u, d):
        return pltpu.make_async_remote_copy(
            src_ref=terms.at[u, d], dst_ref=from_left.at[u, d],
            send_sem=right_send.at[u, d], recv_sem=right_recv.at[u, d],
            device_id={"tensor": lax.rem(z + 1, nz)}, device_id_type=MESH,
        )

    def left_copy(u, d):
        return pltpu.make_async_remote_copy(
            src_ref=terms.at[u, d], dst_ref=from_right.at[u, d],
            send_sem=left_send.at[u, d], recv_sem=left_recv.at[u, d],
            device_id={"tensor": lax.rem(z + nz - 1, nz)}, device_id_type=MESH,
        )

    def add_in(u, d, arrived):
        terms[u, d] = (terms[u, d].astype(jnp.float32) + arrived[u, d].astype(jnp.float32)).astype(jnp.bfloat16)

    units = PARTS * strips

    def when_unit(u, body):
        pl.when(jnp.logical_and(u >= 0, u < units))(functools.partial(body, u))

    def multiply(u):
        h, s = lax.div(u, strips), lax.rem(u, strips)
        pl.when(u < strips)(lambda: weight_copy(u).wait())
        total = jnp.dot(acts[h, 0], held[s, :quarter], preferred_element_type=jnp.float32)
        for q in range(1, nz):
            total += jnp.dot(
                acts[h, q], held[s, q * quarter:(q + 1) * quarter], preferred_element_type=jnp.float32
            )
        for d in range(nz):
            terms[u, d] = total[d * part_rows:(d + 1) * part_rows].astype(jnp.bfloat16)

    def first(u, near):
        @pl.when(z == 0)
        def _():
            for d in (1,) if near else range(nz - 1, 1, -1):
                right_copy(u, d).start()

        @pl.when(z == nz - 1)
        def _():
            for d in (nz - 2,) if near else range(nz - 2):
                left_copy(u, d).start()

    def hop(at, u):
        @pl.when(z == at)
        def _():
            for d in range(nz - 1, at, -1):
                right_copy(u, d).wait_recv()
                add_in(u, d, from_left)
                right_copy(u, d).start()

        @pl.when(z == nz - 1 - at)
        def _():
            for d in range(nz - 1 - at):
                left_copy(u, d).wait_recv()
                add_in(u, d, from_right)
                left_copy(u, d).start()

    def finish(u):
        h, s = lax.div(u, strips), lax.rem(u, strips)
        at = pl.ds(pl.multiple_of(h * part_rows, part_rows), part_rows)
        cols = pl.ds(pl.multiple_of(s * strip, strip), strip)
        own = terms[u, z].astype(jnp.float32)

        @pl.when(z == 0)
        def _():
            left_copy(u, z).wait_recv()
            out[at, cols] = (own + from_right[u, z].astype(jnp.float32)).astype(out.dtype)

        @pl.when(z == nz - 1)
        def _():
            right_copy(u, z).wait_recv()
            out[at, cols] = (own + from_left[u, z].astype(jnp.float32)).astype(out.dtype)

        @pl.when(jnp.logical_and(z > 0, z < nz - 1))
        def _():
            right_copy(u, z).wait_recv()
            left_copy(u, z).wait_recv()
            out[at, cols] = (
                own + from_left[u, z].astype(jnp.float32) + from_right[u, z].astype(jnp.float32)
            ).astype(out.dtype)

    near_lag = strips
    last_lag = max(near_lag + 1, 2 * (nz - 1))

    @pl.loop(0, units + last_lag)
    def _(t):
        for h in range(1, PARTS):
            before = (h - 1) * strips
            pl.when(t == before + CROSS_STEP)(functools.partial(cross, h))
            for k in range(1, nz + 1):
                pl.when(t == before + min(CROSS_STEP + k, strips))(functools.partial(gather, h, k))
        when_unit(t, multiply)
        when_unit(t, lambda u: first(u, False))
        when_unit(t - near_lag, lambda u: first(u, True))
        for at in range(1, nz - 1):
            when_unit(t - 2 * at, functools.partial(hop, at))
        when_unit(t - last_lag, finish)

    for h in range(PARTS):
        for k in range(nz):
            if k > 0:
                mix_copy(h, k).wait_send()
                lev_copy(h, k).wait_send()
            x_copy(h, k).wait_send()
            core_copy(h, k).wait_send()
            pass_copy(h, k).wait_send()

    @pl.loop(0, units)
    def _(u):
        for d in range(nz):
            pl.when(z < d)(lambda d=d: right_copy(u, d).wait_send())
            pl.when(z > d)(lambda d=d: left_copy(u, d).wait_send())


def fused(nz, gathered, tokens, signs, exponents, weights):
    rows, width = tokens.shape
    depth, columns = weights.shape
    quarter = width // nz
    total = rows * gathered
    strip = next(s for s in (1536, 768, 512, 256, 128) if columns % s == 0)
    strips = columns // strip
    units = PARTS * strips
    vmem = pl.BlockSpec(memory_space=pltpu.VMEM)
    return pl.pallas_call(
        functools.partial(kernel, nz, strip),
        out_shape=jax.ShapeDtypeStruct((rows, columns), jnp.bfloat16),
        in_specs=[vmem, vmem, vmem, pl.BlockSpec(memory_space=pl.ANY)],
        out_specs=vmem,
        scratch_shapes=[
            pltpu.VMEM((strips, depth, strip), jnp.bfloat16),
            pltpu.VMEM((nz, rows, quarter), jnp.bfloat16),
            pltpu.VMEM((nz, rows, quarter), jnp.bfloat16),
            pltpu.VMEM((nz, rows, quarter), jnp.bfloat16),
            pltpu.VMEM((PARTS, nz, total // PARTS, quarter), jnp.bfloat16),
        ]
        + [pltpu.VMEM((units, nz, rows // PARTS, strip), jnp.bfloat16)] * 3
        + [
            pltpu.SemaphoreType.DMA((strips,)),
        ]
        + [pltpu.SemaphoreType.DMA((PARTS, nz))] * 10
        + [pltpu.SemaphoreType.DMA((units, nz))] * 4,
        compiler_params=pltpu.CompilerParams(
            collective_id=0, has_side_effects=True, vmem_limit_bytes=60 * 2**20
        ),
        cost_estimate=pl.CostEstimate(
            flops=2 * total * depth * columns, bytes_accessed=2 * depth * columns, transcendentals=0
        ),
    )(tokens, signs[None, :], exponents[None, :], weights)


def shards(tokens, signs, exponents, weights):
    rows, width = tokens.shape
    members = lax.axis_size("tensor")
    gathered = lax.axis_size("dp") * lax.axis_size("pipe")
    if (
        lax.axis_size("dp") == 2 and lax.axis_size("pipe") == 2 and members == gathered
        and width % (BASE * members) == 0 and rows % (16 * PARTS) == 0
        and weights.shape[1] % 128 == 0
        and 2 * width * weights.shape[1] <= 40 * 2**20
    ):
        return fused(members, gathered, tokens, signs, exponents, weights)
    signed = tokens * signs.astype(jnp.bfloat16)[None, :]
    mixed = jnp.dot(
        signed, sylvester(width).astype(jnp.bfloat16), preferred_element_type=jnp.float32
    )
    position = lax.axis_index("tensor")
    for level in range(members.bit_length() - 1):
        partner = partner_2(mixed.astype(jnp.bfloat16), "tensor", level).astype(mixed.dtype)
        upper = position // 2**level % 2
        mixed = jnp.where(upper == 0, mixed + partner, partner - mixed)
    rotated = mixed * jnp.float32(1.0 / math.sqrt(D))
    scale = jnp.exp2(jnp.float32(0.25) * exponents.astype(jnp.float32))[:, None]
    level_value = rotated / scale
    soft = jnp.clip(level_value - jnp.sin(2.0 * math.pi * level_value) / (2.0 * math.pi), -8.0, 7.0)
    quantized = (soft * scale).astype(jnp.bfloat16)
    terms = jnp.dot(
        lax.all_gather(quantized, ("dp", "pipe"), axis=0, tiled=True),
        weights,
        preferred_element_type=jnp.float32,
    )
    summed = lax.psum_scatter(terms.astype(jnp.bfloat16), "tensor", scatter_dimension=0, tiled=True)
    return summed


def solution(mesh):
    placed = (
        P(("groups", "dp", "pipe"), "tensor"),
        P("tensor"),
        P(("groups", "dp", "pipe")),
        P("tensor", ("dp", "pipe")),
    )
    return jax.shard_map(
        shards,
        mesh=mesh,
        in_specs=placed,
        out_specs=P(("groups", "tensor"), ("dp", "pipe")),
        check_vma=False,
    )
```

```python
import functools
import math

import jax
import jax.numpy as jnp
from jax import lax
from jax.experimental import pallas as pl
from jax.experimental.pallas import tpu as pltpu
from jax.sharding import PartitionSpec as P

D = 16384
MESH = pl.DeviceIdType.MESH
BASE = 256
PARTS = 2
CROSS_STEP = 0


def partner_2(value, axis, bit):
    mask = 2**bit
    pairs = [(source, source ^ mask) for source in range(lax.axis_size(axis))]
    return lax.ppermute(value, axis, pairs)


def sylvester(order):
    rows = lax.broadcasted_iota(jnp.int32, (order, order), 0)
    cols = lax.broadcasted_iota(jnp.int32, (order, order), 1)
    both = rows & cols
    shift = 1
    while shift < order.bit_length():
        both = both ^ (both >> shift)
        shift *= 2
    return (1 - 2 * (both & 1)).astype(jnp.float32)


def butterfly(values):
    values = list(values)
    step = 1
    while step < len(values):
        for low in range(len(values)):
            if low & step == 0:
                a, b = values[low], values[low + step]
                values[low], values[low + step] = a + b, a - b
        step *= 2
    return values


def sin_turns(turns):
    part = turns - jnp.round(turns)
    part = jnp.where(part > 0.25, 0.5 - part, jnp.where(part < -0.25, -0.5 - part, part))
    angle = part * jnp.float32(2.0 * math.pi)
    square = angle * angle
    total = jnp.float32(-1.0 / math.factorial(11))
    for order, sign in ((9, 1.0), (7, -1.0), (5, 1.0), (3, -1.0)):
        total = total * square + jnp.float32(sign / math.factorial(order))
    return angle + angle * square * total


def fake_quantize(rotated, scale, inverse):
    level = rotated * inverse
    soft = jnp.clip(level - sin_turns(level) * jnp.float32(1.0 / (2.0 * math.pi)), -8.0, 7.0)
    return (soft * scale).astype(jnp.bfloat16)


def kernel(
    nz, strip, tokens, signs, exponents, weights, out,
    held, mixed, taken, levels, acts, terms, from_left, from_right,
    weight_sem, mix_send, mix_recv, lev_send, lev_recv, x_send, x_recv,
    core_send, core_recv, pass_send, pass_recv, right_send, right_recv, left_send, left_recv,
):
    rows, width = tokens.shape
    quarter = width // nz
    part_rows = rows // PARTS
    strips = weights.shape[1] // strip
    z = lax.axis_index("tensor")
    x = lax.axis_index("dp")
    core = lax.axis_index("pipe")
    across = {"dp": 1 - x}
    beside = {"pipe": 1 - core}

    def weight_copy(s):
        return pltpu.make_async_copy(
            weights.at[:, pl.ds(pl.multiple_of(s * strip, strip), strip)], held.at[s], weight_sem.at[s]
        )

    barrier = pltpu.get_barrier_semaphore()
    for k in range(1, nz):
        pl.semaphore_signal(barrier, inc=1, device_id={"tensor": z ^ k}, device_id_type=MESH)
    pl.semaphore_signal(barrier, inc=1, device_id=across, device_id_type=MESH)
    pl.semaphore_signal(barrier, inc=1, device_id=beside, device_id_type=MESH)

    small = sylvester(BASE).astype(jnp.bfloat16)
    signed = signs[...].astype(jnp.bfloat16)

    def mix_copy(h, k):
        span = pl.ds(h * part_rows, part_rows)
        return pltpu.make_async_remote_copy(
            src_ref=mixed.at[z ^ k, span], dst_ref=taken.at[z, span],
            send_sem=mix_send.at[h, k], recv_sem=mix_recv.at[h, k],
            device_id={"tensor": z ^ k}, device_id_type=MESH,
        )

    def start_mix(h):
        for k in range(nz - 1, 0, -1):
            mix_copy(h, k).start()

    def mix(h):
        span = slice(h * part_rows, (h + 1) * part_rows)
        blocks = []
        for a in range(width // BASE):
            cols = slice(a * BASE, (a + 1) * BASE)
            blocks.append(jnp.dot(tokens[span, cols] * signed[:, cols], small, preferred_element_type=jnp.float32))
        for a, block in enumerate(butterfly(blocks)):
            q, at = divmod(a * BASE, quarter)
            mixed[q, span, at:at + BASE] = (block * jnp.float32(1.0 / math.sqrt(D))).astype(jnp.bfloat16)
        taken[z, span] = mixed[z, span]

    mix(0)
    pl.semaphore_wait(barrier, nz + 1)
    start_mix(0)
    pl.loop(0, strips)(lambda s: weight_copy(s).start())
    for h in range(1, PARTS):
        mix(h)

    at_row = lax.broadcasted_iota(jnp.int32, (rows, rows), 0)
    at_col = lax.broadcasted_iota(jnp.int32, (rows, rows), 1)
    power = jnp.sum(
        jnp.where(at_row == at_col, 0.25 * exponents[...].astype(jnp.float32), 0.0), axis=1, keepdims=True
    )
    scale = jnp.exp2(power)
    inverse = jnp.exp2(-power)

    def rows_of(owner_x):
        return pl.ds(pl.multiple_of((owner_x * 2 + core) * part_rows, part_rows), part_rows)

    def lev_copy(h, k):
        return pltpu.make_async_remote_copy(
            src_ref=levels.at[z ^ k, pl.ds(h * part_rows, part_rows)], dst_ref=acts.at[h, z, rows_of(x)],
            send_sem=lev_send.at[h, k], recv_sem=lev_recv.at[h, k],
            device_id={"tensor": z ^ k}, device_id_type=MESH,
        )

    def side_copy(h, k, owner_x, target, send, recv):
        ref = acts.at[h, z ^ k, rows_of(owner_x)]
        return pltpu.make_async_remote_copy(
            src_ref=ref, dst_ref=ref, send_sem=send.at[h, k], recv_sem=recv.at[h, k],
            device_id=target, device_id_type=MESH,
        )

    def x_copy(h, k):
        return side_copy(h, k, x, across, x_send, x_recv)

    def core_copy(h, k):
        return side_copy(h, k, x, beside, core_send, core_recv)

    def pass_copy(h, k):
        return side_copy(h, k, 1 - x, beside, pass_send, pass_recv)

    def cross(h):
        span = slice(h * part_rows, (h + 1) * part_rows)
        for k in range(1, nz):
            mix_copy(h, k).wait_recv()
        for lane in range(0, quarter, BASE):
            lanes = slice(lane, lane + BASE)
            whole = butterfly([taken[q, span, lanes].astype(jnp.float32) for q in range(nz)])
            for q in range(nz):
                levels[q, span, lanes] = fake_quantize(whole[q], scale[span], inverse[span])
        for k in range(nz - 1, 0, -1):
            lev_copy(h, k).start()
        acts[h, z, rows_of(x)] = levels[z, span]
        x_copy(h, 0).start()
        core_copy(h, 0).start()
        if h + 1 < PARTS:
            start_mix(h + 1)

    def gather(h, k):
        if k < nz:
            lev_copy(h, k).wait_recv()
            x_copy(h, k).start()
            core_copy(h, k).start()
        x_copy(h, k - 1).wait_recv()
        pass_copy(h, k - 1).start()
        if k == nz:
            for i in range(nz):
                core_copy(h, i).wait_recv()
                pass_copy(h, i).wait_recv()

    cross(0)
    for k in range(1, nz + 1):
        gather(0, k)

    def right_copy(u, d):
        return pltpu.make_async_remote_copy(
            src_ref=terms.at[u, d], dst_ref=from_left.at[u, d],
            send_sem=right_send.at[u, d], recv_sem=right_recv.at[u, d],
            device_id={"tensor": lax.rem(z + 1, nz)}, device_id_type=MESH,
        )

    def left_copy(u, d):
        return pltpu.make_async_remote_copy(
            src_ref=terms.at[u, d], dst_ref=from_right.at[u, d],
            send_sem=left_send.at[u, d], recv_sem=left_recv.at[u, d],
            device_id={"tensor": lax.rem(z + nz - 1, nz)}, device_id_type=MESH,
        )

    def add_in(u, d, arrived):
        terms[u, d] = (terms[u, d].astype(jnp.float32) + arrived[u, d].astype(jnp.float32)).astype(jnp.bfloat16)

    units = PARTS * strips

    def when_unit(u, body):
        pl.when(jnp.logical_and(u >= 0, u < units))(functools.partial(body, u))

    def multiply(u):
        h, s = lax.div(u, strips), lax.rem(u, strips)
        pl.when(u < strips)(lambda: weight_copy(u).wait())
        total = jnp.dot(acts[h, 0], held[s, :quarter], preferred_element_type=jnp.float32)
        for q in range(1, nz):
            total += jnp.dot(
                acts[h, q], held[s, q * quarter:(q + 1) * quarter], preferred_element_type=jnp.float32
            )
        for d in range(nz):
            terms[u, d] = total[d * part_rows:(d + 1) * part_rows].astype(jnp.bfloat16)

    def first(u, near):
        @pl.when(z == 0)
        def _():
            for d in (1,) if near else range(nz - 1, 1, -1):
                right_copy(u, d).start()

        @pl.when(z == nz - 1)
        def _():
            for d in (nz - 2,) if near else range(nz - 2):
                left_copy(u, d).start()

    def hop(at, u):
        @pl.when(z == at)
        def _():
            for d in range(nz - 1, at, -1):
                right_copy(u, d).wait_recv()
                add_in(u, d, from_left)
                right_copy(u, d).start()

        @pl.when(z == nz - 1 - at)
        def _():
            for d in range(nz - 1 - at):
                left_copy(u, d).wait_recv()
                add_in(u, d, from_right)
                left_copy(u, d).start()

    def finish(u):
        h, s = lax.div(u, strips), lax.rem(u, strips)
        at = pl.ds(pl.multiple_of(h * part_rows, part_rows), part_rows)
        cols = pl.ds(pl.multiple_of(s * strip, strip), strip)
        own = terms[u, z].astype(jnp.float32)

        @pl.when(z == 0)
        def _():
            left_copy(u, z).wait_recv()
            out[at, cols] = (own + from_right[u, z].astype(jnp.float32)).astype(out.dtype)

        @pl.when(z == nz - 1)
        def _():
            right_copy(u, z).wait_recv()
            out[at, cols] = (own + from_left[u, z].astype(jnp.float32)).astype(out.dtype)

        @pl.when(jnp.logical_and(z > 0, z < nz - 1))
        def _():
            right_copy(u, z).wait_recv()
            left_copy(u, z).wait_recv()
            out[at, cols] = (
                own + from_left[u, z].astype(jnp.float32) + from_right[u, z].astype(jnp.float32)
            ).astype(out.dtype)

    near_lag = strips
    last_lag = max(near_lag + 1, nz)

    @pl.loop(0, units + last_lag)
    def _(t):
        for h in range(1, PARTS):
            before = (h - 1) * strips
            pl.when(t == before + CROSS_STEP)(functools.partial(cross, h))
            for k in range(1, nz + 1):
                pl.when(t == before + min(CROSS_STEP + k, strips))(functools.partial(gather, h, k))
        when_unit(t, multiply)
        when_unit(t, lambda u: first(u, False))
        when_unit(t - near_lag, lambda u: first(u, True))
        for at in range(1, nz - 1):
            when_unit(t - at, functools.partial(hop, at))
        when_unit(t - last_lag, finish)

    for h in range(PARTS):
        for k in range(nz):
            if k > 0:
                mix_copy(h, k).wait_send()
                lev_copy(h, k).wait_send()
            x_copy(h, k).wait_send()
            core_copy(h, k).wait_send()
            pass_copy(h, k).wait_send()

    @pl.loop(0, units)
    def _(u):
        for d in range(nz):
            pl.when(z < d)(lambda d=d: right_copy(u, d).wait_send())
            pl.when(z > d)(lambda d=d: left_copy(u, d).wait_send())


def fused(nz, gathered, tokens, signs, exponents, weights):
    rows, width = tokens.shape
    depth, columns = weights.shape
    quarter = width // nz
    total = rows * gathered
    strip = next(s for s in (1536, 768, 512, 256, 128) if columns % s == 0)
    strips = columns // strip
    units = PARTS * strips
    vmem = pl.BlockSpec(memory_space=pltpu.VMEM)
    return pl.pallas_call(
        functools.partial(kernel, nz, strip),
        out_shape=jax.ShapeDtypeStruct((rows, columns), jnp.bfloat16),
        in_specs=[vmem, vmem, vmem, pl.BlockSpec(memory_space=pl.ANY)],
        out_specs=vmem,
        scratch_shapes=[
            pltpu.VMEM((strips, depth, strip), jnp.bfloat16),
            pltpu.VMEM((nz, rows, quarter), jnp.bfloat16),
            pltpu.VMEM((nz, rows, quarter), jnp.bfloat16),
            pltpu.VMEM((nz, rows, quarter), jnp.bfloat16),
            pltpu.VMEM((PARTS, nz, total // PARTS, quarter), jnp.bfloat16),
        ]
        + [pltpu.VMEM((units, nz, rows // PARTS, strip), jnp.bfloat16)] * 3
        + [
            pltpu.SemaphoreType.DMA((strips,)),
        ]
        + [pltpu.SemaphoreType.DMA((PARTS, nz))] * 10
        + [pltpu.SemaphoreType.DMA((units, nz))] * 4,
        compiler_params=pltpu.CompilerParams(
            collective_id=0, has_side_effects=True, vmem_limit_bytes=60 * 2**20
        ),
        cost_estimate=pl.CostEstimate(
            flops=2 * total * depth * columns, bytes_accessed=2 * depth * columns, transcendentals=0
        ),
    )(tokens, signs[None, :], exponents[None, :], weights)


def shards(tokens, signs, exponents, weights):
    rows, width = tokens.shape
    members = lax.axis_size("tensor")
    gathered = lax.axis_size("dp") * lax.axis_size("pipe")
    if (
        lax.axis_size("dp") == 2 and lax.axis_size("pipe") == 2 and members == gathered
        and width % (BASE * members) == 0 and rows % (16 * PARTS) == 0
        and weights.shape[1] % 128 == 0
        and 2 * width * weights.shape[1] <= 40 * 2**20
    ):
        return fused(members, gathered, tokens, signs, exponents, weights)
    signed = tokens * signs.astype(jnp.bfloat16)[None, :]
    mixed = jnp.dot(
        signed, sylvester(width).astype(jnp.bfloat16), preferred_element_type=jnp.float32
    )
    position = lax.axis_index("tensor")
    for level in range(members.bit_length() - 1):
        partner = partner_2(mixed.astype(jnp.bfloat16), "tensor", level).astype(mixed.dtype)
        upper = position // 2**level % 2
        mixed = jnp.where(upper == 0, mixed + partner, partner - mixed)
    rotated = mixed * jnp.float32(1.0 / math.sqrt(D))
    scale = jnp.exp2(jnp.float32(0.25) * exponents.astype(jnp.float32))[:, None]
    level_value = rotated / scale
    soft = jnp.clip(level_value - jnp.sin(2.0 * math.pi * level_value) / (2.0 * math.pi), -8.0, 7.0)
    quantized = (soft * scale).astype(jnp.bfloat16)
    terms = jnp.dot(
        lax.all_gather(quantized, ("dp", "pipe"), axis=0, tiled=True),
        weights,
        preferred_element_type=jnp.float32,
    )
    summed = lax.psum_scatter(terms.astype(jnp.bfloat16), "tensor", scatter_dimension=0, tiled=True)
    return summed


def solution(mesh):
    placed = (
        P(("groups", "dp", "pipe"), "tensor"),
        P("tensor"),
        P(("groups", "dp", "pipe")),
        P("tensor", ("dp", "pipe")),
    )
    return jax.shard_map(
        shards,
        mesh=mesh,
        in_specs=placed,
        out_specs=P(("groups", "tensor"), ("dp", "pipe")),
        check_vma=False,
    )
```
